512 devices in a mesh: leaf: 32 (over x, z), rows: 16 (over y, core).
Axes of the slice: x: 4, y: 8, z: 8, core: 2. Of those that a mesh axis runs over, the one named last changes fastest.
Arguments:
- basis: bfloat16 [32, 16384, 256], P('leaf', 'rows'), may hold values from -0.046875 to 0.046875
- stiff: bfloat16 [32, 16384, 1664], P('leaf', 'rows'), may hold values from -6 to 6
- kcols: int32 [32, 256, 26], P('leaf', 'rows'), may hold values from 0 to 255
- couple: bfloat16 [32, 16384, 128], P('leaf', 'rows'), may hold values from -48 to 48
- links: int32 [32, 256, 2], P('leaf', 'rows'), may hold values from 0 to 15
- shift: float32 [32, 16384], P('leaf', 'rows'), may hold values from 1 to 10
- mass: float32 [32, 16384], P('leaf', 'rows'), may hold values from 0.5 to 4
Outputs:
- kred: float32 [32, 256, 1024], P('leaf', None, 'rows')
- mred: float32 [32, 256, 256], P('leaf', None, 'rows')
The draws below stay inside these ranges and needn't reach their ends.
All inputs are finite; a program needn't handle non-finite values.
Results may differ from the reference program's by a relative error of at most 0.0028.
Values may be sent and summed in bfloat16 or wider, within the bound.
No kernel may reach another device: no remote copies, remote signals or barrier semaphores. Data moves between devices by JAX's collectives and lax.ppermute only.
A program may use at most 128 MiB of HBM per device.

```python
import math
import jax
import jax.numpy as jnp
from jax import lax

BLK = 64
KM = 256
NB = 26
ROWS_DEV = 1024
ROWS = 16384
BLOCKS = 256
SUBS = 32


def with_ends(values, own_key, low, high):
    longest = values.shape.index(max(values.shape))
    spots = []
    for shift in (0, 1):
        where = [jax.random.randint(jax.random.fold_in(own_key, axis), (), 0, length) for axis, length in enumerate(values.shape)]
        where[longest] = (where[longest] + shift) % values.shape[longest]
        spots.append(tuple(where))
    return values.at[spots[0]].set(low).at[spots[1]].set(high)


def level_of(rng, shape, cuts, least, high):
    factor_of, own = 1.0, jax.random.fold_in(rng, 6)
    for position, blocks in cuts:
        heights = jnp.exp(jax.random.uniform(jax.random.fold_in(own, position), (blocks,), jnp.float32, least / len(cuts), high / len(cuts)))
        factor_of = factor_of * jnp.repeat(heights, shape[position] // blocks).reshape([-1 if axis == position else 1 for axis in range(len(shape))])
    return factor_of


def centred(own_key, dims, width, most, split=(), kind=jnp.bfloat16):
    factor_of = level_of(own_key, dims, split, -0.22, 0.18) if split else 1.0
    entries = jax.random.normal(own_key, dims, jnp.float32) * width * factor_of
    return jnp.minimum(jnp.maximum(entries, -most), most).astype(kind)


def setup_inputs(seed: int = 0) -> dict:
    key_of = jax.random.split(jax.random.key(seed), 8)
    return {
        "basis": centred(key_of[0], (SUBS, ROWS, KM), (ROWS ** -0.5), 0.046875, ((0, 32), (1, 16))),
        "stiff": centred(key_of[1], (SUBS, ROWS, NB * BLK), 1.0, 6.0, ((0, 32), (1, 16))),
        "kcols": with_ends(jax.random.randint(key_of[2], (SUBS, BLOCKS, NB), 0, BLOCKS), jax.random.fold_in(key_of[2], 1), 0, BLOCKS - 1).astype(jnp.int32),
        "couple": centred(key_of[3], (SUBS, ROWS, 2 * BLK), 8.0, 48.0, ((0, 32), (1, 16))),
        "links": with_ends(jax.random.randint(key_of[4], (SUBS, BLOCKS, 2), 0, ROWS_DEV // BLK), jax.random.fold_in(key_of[4], 1), 0, (ROWS_DEV // BLK) - 1).astype(jnp.int32),
        "shift": jnp.clip(jnp.exp(math.log(10.0) - 2.3025851 * jax.random.uniform(key_of[5], (SUBS, ROWS), jnp.float32) ** level_of(key_of[5], (SUBS, ROWS), ((0, 32), (1, 16)), -0.2, 0.2)), 1.0, 10.0),
        "mass": jnp.clip(jnp.exp(math.log(4.0) - 2.0794415 * jax.random.uniform(key_of[6], (SUBS, ROWS), jnp.float32) ** level_of(key_of[6], (SUBS, ROWS), ((0, 32), (1, 16)), -0.2, 0.2)), 0.5, 4.0),
    }


def reference(basis, stiff, kcols, couple, links, shift, mass):
    shard_blocks = ROWS_DEV // BLK
    rows_total = basis.shape[1]
    nblocks = rows_total // BLK
    base_rows = (jnp.arange(nblocks, dtype=jnp.int32) // shard_blocks) * shard_blocks

    def one_sub(sub):
        local_basis = basis[sub]
        table = local_basis.reshape(nblocks, BLK, KM)
        picked = jnp.take(table, kcols[sub], axis=0).reshape(nblocks, NB * BLK, KM).astype(jnp.float32)
        smat = stiff[sub].reshape(nblocks, BLK, NB * BLK).astype(jnp.float32)
        image = jnp.einsum("bij,bjm->bim", smat, picked).reshape(rows_total, KM)
        image = (image + shift[sub][:, None] * local_basis.astype(jnp.float32)).astype(jnp.bfloat16)
        terms = [jnp.dot(local_basis.T, image, preferred_element_type=jnp.float32)]
        for which in range(2):
            partner = basis[jnp.bitwise_xor(sub, which + 1)].reshape(nblocks, BLK, KM)
            index = (base_rows + links[sub][:, which]).astype(jnp.int32)
            partner_rows = jnp.take(partner, index, axis=0).astype(jnp.float32)
            cmat = couple[sub][:, which * BLK:(which + 1) * BLK].reshape(nblocks, BLK, BLK).astype(jnp.float32)
            coupled = jnp.einsum("bij,bjm->bim", cmat, partner_rows).reshape(rows_total, KM).astype(jnp.bfloat16)
            terms.append(jnp.dot(local_basis.T, coupled, preferred_element_type=jnp.float32))
        terms.append(jnp.zeros((KM, KM), jnp.float32))
        stacked = jnp.stack(terms)
        order = jnp.bitwise_xor(jnp.arange(4, dtype=jnp.int32), (sub % 4).astype(jnp.int32))
        row_block = jnp.take(stacked, order, axis=0).transpose(1, 0, 2).reshape(KM, 4 * KM)
        weighted = (mass[sub][:, None] * local_basis.astype(jnp.float32)).astype(jnp.bfloat16)
        mass_block = jnp.dot(local_basis.T, weighted, preferred_element_type=jnp.float32)
        return row_block, mass_block

    kred, mred = lax.map(one_sub, jnp.arange(SUBS, dtype=jnp.int32))
    return kred, mred
```

```python
import functools

import jax
import jax.numpy as jnp
from jax import lax
from jax.experimental import pallas as pl
from jax.experimental.pallas import tpu as pltpu
from jax.sharding import PartitionSpec as P

F32, BF16 = jnp.float32, jnp.bfloat16
BLK = 64
MIB = 2**20
COUPLE, SHIFT, MASS, KCOLS, LINKS, AUX = 0, 1024, 1032, 1040, 1056, 1072
VMEM = pl.BlockSpec(memory_space=pltpu.VMEM)
SMEM = pl.BlockSpec(memory_space=pltpu.SMEM)
ANY = pl.BlockSpec(memory_space=pl.ANY)
HBM = pl.BlockSpec(memory_space=pltpu.HBM)


def place():
    row = lax.axis_index("rows")
    return row // 4, (row // 2) % 2, row % 2


def send(value, to):
    leaves, rows = lax.axis_size("leaf"), lax.axis_size("rows")
    pairs = []
    for leaf in range(leaves):
        for row in range(rows):
            target = to(leaf, row)
            if target is not None:
                pairs.append((leaf * rows + row, target[0] * rows + target[1]))
    return lax.ppermute(value, ("leaf", "rows"), pairs)


def to_core(leaf, row):
    return leaf, row ^ 1


def to_side(leaf, row):
    return leaf, row ^ 2


def ring(forward):
    def to(leaf, row):
        step = 2 if (row % 2 == 0) == forward else -2
        return leaf, (row + step) % 16

    return to


def to_group(mask):
    return lambda leaf, row: (leaf, row ^ (4 * mask))


def to_own_group(mask):
    def to(leaf, row):
        return (leaf, 4 * (leaf % 4) + row % 4) if row // 4 == (leaf % 4) ^ mask else None

    return to


def call(body, outs, arrays, far=(), scratch=(), flops=0, vmem=8, aliases=None):
    moved = sum(x.size * x.dtype.itemsize for x in [*arrays, *far, *outs])
    return pl.pallas_call(
        body,
        out_shape=outs,
        in_specs=[VMEM] * len(arrays) + [HBM] * len(far),
        out_specs=[VMEM] * len(outs),
        scratch_shapes=list(scratch),
        input_output_aliases=aliases or {},
        compiler_params=pltpu.CompilerParams(vmem_limit_bytes=vmem * MIB),
        cost_estimate=pl.CostEstimate(flops=flops, bytes_accessed=moved, transcendentals=0),
    )(*arrays, *far)


def fetch(pairs, sems):
    copies = [pltpu.make_async_copy(src, dst, sems.at[n]) for n, (src, dst) in enumerate(pairs)]
    for copy in copies:
        copy.start()
    return copies


def shape(*dims, dtype=F32):
    return jax.ShapeDtypeStruct(dims, dtype)


def mine_of(width, column):
    here = lax.broadcasted_iota(jnp.int32, (width, 128), 0)
    want = column(lax.broadcasted_iota(jnp.int32, (width, 128), 1))
    return (here == want).astype(F32).astype(BF16)


def dot(a, b):
    return jnp.dot(a, b, preferred_element_type=F32)


def dot_t(a, b):
    return lax.dot_general(a, b, (((0,), (0,)), ((), ())), preferred_element_type=F32)


def after(value, *others):
    return lax.optimization_barrier((value, *others))[0]


def aux_kernel(couple_at, kcols_at, links_at, shift_at, mass_at, out, couple, kcols, links, shift, mass, sems):
    held = (couple, kcols, links, shift, mass)
    for copy in fetch(zip((couple_at, kcols_at, links_at, shift_at, mass_at), held), sems):
        copy.wait()
    out[COUPLE : COUPLE + 1024, :] = couple[0].astype(F32)
    for k in range(8):
        out[SHIFT + k : SHIFT + k + 1, :] = shift[:, k * 128 : (k + 1) * 128]
        out[MASS + k : MASS + k + 1, :] = mass[:, k * 128 : (k + 1) * 128]
    out[KCOLS:AUX, :] = jnp.zeros((AUX - KCOLS, 128), F32)
    out[KCOLS : KCOLS + 16, 0:26] = kcols[0].astype(F32)
    out[LINKS : LINKS + 2, 0:16] = links[0].astype(F32)


def half_kernel(own, other, out, both):
    _, _, core = place()
    pick = mine_of(256, lambda n: 64 * core + n + jnp.where(n >= 64, 64, 0))
    out[pl.ds(pl.multiple_of(core * 1024, 1024), 1024), :] = dot(own[...], pick).astype(BF16)
    out[pl.ds(pl.multiple_of((1 - core) * 1024, 1024), 1024), :] = dot(other[...], pick).astype(BF16)
    both[0:1024, :] = own[...]
    both[1024:2048, :] = other[...]


def spread(dst, rows_own, rows_other):
    for part, rows in enumerate((rows_own, rows_other)):
        turned = jnp.transpose(jnp.concatenate([rows, jnp.zeros((120, 128), F32)], axis=0))
        for k in range(8):
            dst[part * 1024 + k * 128 : part * 1024 + (k + 1) * 128, :] = jnp.broadcast_to(
                turned[:, k : k + 1], (128, 128)
            )


def early_kernel(both, aux, aux_other, partner, to_send, to_keep, mred, coupled, weights, masked, spots, at, sem):
    _, _, core = place()
    spots[...] = jnp.zeros((8, 128), jnp.int32)
    for part, rows in enumerate((aux, aux_other)):
        links = rows[LINKS : LINKS + 2, 0:16].astype(jnp.int32)
        spots[part : part + 1, 0:16] = part * 1024 + jnp.where(core == 0, links[0:1, :], links[1:2, :]) * BLK
    copy = pltpu.make_async_copy(spots, at, sem)
    copy.start()
    mine = lax.broadcasted_iota(jnp.int32, (1024, 128), 1) // BLK == core
    for part, rows in enumerate((aux, aux_other)):
        couple = rows[COUPLE : COUPLE + 1024, :]
        masked[part * 1024 : (part + 1) * 1024, :] = jnp.where(mine, couple, 0.0).astype(BF16)
    copy.wait()

    def one(b, carry):
        rows = pl.ds(pl.multiple_of(b * BLK, BLK), BLK)
        block = partner[pl.ds(pl.multiple_of(at[b // 16, b % 16], BLK), BLK), :]
        coupled[rows, :] = dot(masked[rows, :], jnp.concatenate([block, block], axis=0)).astype(BF16)
        return carry

    lax.fori_loop(0, 32, one, 0, unroll=8)
    spread(weights, aux[MASS : MASS + 8, :], aux_other[MASS : MASS + 8, :])
    pick = mine_of(256, lambda n: 64 * ((n % 64) // 16) + 32 * (n // 64) + 16 * core + n % 16)
    weighted = (weights[...] * dot(both[...], pick)).astype(BF16)
    mred[...] = dot_t(weighted, both[...])
    term = dot_t(coupled[...], both[...])
    for k in range(2):
        low, high = term[k * 128 : k * 128 + 64, :], term[k * 128 + 64 : k * 128 + 128, :]
        to_keep[k * 64 : (k + 1) * 64, :] = jnp.where(core == 0, low, high)
        to_send[k * 64 : (k + 1) * 64, :] = jnp.where(core == 0, high, low)


def turn_kernel(kept, came, mred, to_send, to_keep):
    _, side, core = place()
    sib = jnp.where(core == 0, kept[...], came[...])
    cous = jnp.where(core == 0, came[...], kept[...])
    for t, term in enumerate((sib, cous, mred[...])):
        low, high = term[0:64, :], term[64:128, :]
        to_send[t * 64 : (t + 1) * 64, :] = jnp.where(side == 0, high, low)
        to_keep[t * 64 : (t + 1) * 64, :] = jnp.where(side == 0, low, high)


def split_kernel(kept, came, to_send, to_keep):
    group, _, _ = place()
    odd = (group ^ (lax.axis_index("leaf") % 4)) % 2 == 1
    sib = kept[0:64, :] + came[0:64, :]
    cous = kept[64:128, :] + came[64:128, :]
    mass = kept[128:192, :] + came[128:192, :]
    to_keep[0:64, :] = jnp.where(odd, sib, cous)
    to_send[0:64, :] = jnp.where(odd, cous, sib)
    low = group % 2 == 0
    for k in range(2):
        even, uneven = mass[k * 32 : k * 32 + 16, :], mass[k * 32 + 16 : k * 32 + 32, :]
        to_keep[64 + k * 16 : 80 + k * 16, :] = jnp.where(low, even, uneven)
        to_send[64 + k * 16 : 80 + k * 16, :] = jnp.where(low, uneven, even)


def stage_kernel(both, aux, aux_other, *refs):
    kcols_at, stiff, stiff_other = refs[:3]
    pieces = refs[3:10]
    table, matrix, start, spots, kcols, sems = refs[10:]
    _, _, core = place()
    chip = lax.axis_index("rows") // 2
    places = [2048 * d for d in (0, 7, 1, 6, 2, 5, 3)]
    pairs = [(kcols_at, kcols), (pieces[0], table.at[0:2048, :])]
    pairs += [(piece, table.at[lo : lo + 2048, :]) for piece, lo in list(zip(pieces, places))[1:]]
    pairs += [(stiff.at[0], matrix.at[0:1024, :]), (stiff_other, matrix.at[1024:2048, :])]
    copies = fetch(pairs, sems)
    spread(start, aux[SHIFT : SHIFT + 8, :], aux_other[SHIFT : SHIFT + 8, :])
    copies[0].wait()
    copies[1].wait()
    spots[...] = jnp.zeros((32, 128), jnp.int32)
    for part in range(2):
        column = kcols[0] if part == 0 else aux_other[KCOLS : KCOLS + 16, 0:26].astype(jnp.int32)
        ahead = column // 32 - chip
        ahead = jnp.where(core == 0, ahead, -ahead) & 7
        spots[part * 16 : (part + 1) * 16, 0:26] = ahead * 2048 + (column % 32) * BLK
    for part in range(2):
        rows = slice(part * 1024, (part + 1) * 1024)
        mine = pl.ds(pl.multiple_of((part * 1024 + core * 1024) % 2048, 1024), 1024)
        start[rows, :] = start[rows, :] * table[mine, :].astype(F32)
    for copy in copies[2:]:
        copy.wait()


def own_kernel(table, matrix, start, spots, both, last_at, to_send, to_keep, full, image, at, sems):
    _, side, _ = place()
    copies = fetch([(spots, at), (last_at, full.at[4 * 2048 : 5 * 2048, :])], sems)
    for copy in copies:
        copy.wait()

    def one(b, carry):
        rows = pl.ds(pl.multiple_of(b * BLK, BLK), BLK)
        total = start[rows, :]
        blocks = [full[pl.ds(pl.multiple_of(at[b, k], BLK), BLK), :] for k in range(26)]
        for g in range(0, 26, 4):
            picked = jnp.concatenate(blocks[g : g + 4], axis=0)
            width = picked.shape[0]
            total += dot(matrix[rows, g * BLK : g * BLK + width], picked)
        image[rows, :] = total.astype(BF16)
        return carry

    lax.fori_loop(0, 32, one, 0, unroll=8)
    result = dot_t(image[...], both[...])
    low, high = result[0:64, :], result[64:128, :]
    to_send[...] = jnp.where(side == 0, high, low)
    to_keep[...] = jnp.where(side == 0, low, high)


def gather_kernel(kept, came, early_kept, early_came, total, pay, base, mass_base):
    group, _, _ = place()
    term = group ^ (lax.axis_index("leaf") % 4)
    own = kept[...] + came[...]
    early = early_kept[0:64, :] + early_came[0:64, :]
    total[...] = own
    zero = jnp.zeros_like(own)
    pay[0:64, :] = jnp.where(term == 2, own, jnp.where(term == 1, zero, early))
    base[...] = jnp.where(term == 0, own, jnp.where(term == 3, zero, early))
    first = early_kept[64:80, :] + early_came[64:80, :]
    second = early_kept[80:96, :] + early_came[80:96, :]
    low = group < 2
    pay[64:80, :] = jnp.where(low, second, first)
    mass_base[...] = jnp.where(low, first, second)


def last_kernel(base, mass_base, one, two, three, kred, mred):
    kred[...] = base[...] + one[...] + two[0:64, :] + three[...]
    mred[...] = mass_base[...] + two[64:80, :]


def shards(basis, stiff, kcols, couple, links, shift, mass):
    own = basis[0]
    links = links.transpose(0, 2, 1)
    other = send(own, to_core)
    half, both = call(half_kernel, [shape(2048, 128, dtype=BF16), shape(2048, 256, dtype=BF16)], [own, other])
    left1 = send(half, ring(True))
    (aux,) = call(
        aux_kernel,
        [shape(AUX, 128)],
        [],
        [couple, after(kcols, half), links, shift, mass],
        [
            pltpu.VMEM((1, 1024, 128), BF16),
            pltpu.VMEM((1, 16, 26), jnp.int32),
            pltpu.VMEM((1, 2, 16), jnp.int32),
            pltpu.VMEM((1, 1024), F32),
            pltpu.VMEM((1, 1024), F32),
            pltpu.SemaphoreType.DMA((5,)),
        ],
    )
    right1 = send(after(half, aux), ring(False))
    partner = send(both, lambda leaf, row: (leaf ^ (1 + row % 2), row))
    stiff_other = send(stiff[0], to_core)
    aux_other = send(after(aux, stiff_other), to_core)
    left2, right2 = send(left1, ring(True)), send(right1, ring(False))
    left3, right3 = send(left2, ring(True)), send(right2, ring(False))
    left4 = send(left3, ring(True))
    go, keep, mass_part = call(
        early_kernel,
        [shape(128, 256)] * 3,
        [both, aux, aux_other, partner],
        [],
        [
            pltpu.VMEM((2048, 256), BF16),
            pltpu.VMEM((2048, 128), F32),
            pltpu.VMEM((2048, 128), BF16),
            pltpu.VMEM((8, 128), jnp.int32),
            pltpu.SMEM((8, 128), jnp.int32),
            pltpu.SemaphoreType.DMA,
        ],
        flops=2**30,
        vmem=16,
    )
    came = send(go, to_core)
    go, keep = call(turn_kernel, [shape(192, 256)] * 2, [keep, came, mass_part])
    came = send(go, to_side)
    go, early_keep = call(split_kernel, [shape(96, 256)] * 2, [keep, came])
    early_came = send(go, to_group(1))

    table, matrix, start, spots = call(
        stage_kernel,
        [shape(16384, 128, dtype=BF16), shape(2048, 1664, dtype=BF16), shape(2048, 128), shape(32, 128, dtype=jnp.int32)],
        [both, aux, aux_other],
        [kcols, stiff, stiff_other, half, left1, right1, left2, right2, left3, right3],
        [pltpu.VMEM((1, 16, 26), jnp.int32), pltpu.SemaphoreType.DMA((10,))],
    )
    go, keep, _ = call(
        own_kernel,
        [shape(64, 256), shape(64, 256), shape(16384, 128, dtype=BF16)],
        [table, matrix, start, spots, both],
        [left4],
        [pltpu.VMEM((2048, 128), BF16), pltpu.SMEM((32, 128), jnp.int32), pltpu.SemaphoreType.DMA((2,))],
        flops=2**30,
        aliases={0: 2},
    )
    came = send(go, to_side)
    total, pay, base, mass_base = call(
        gather_kernel,
        [shape(64, 256), shape(80, 256), shape(64, 256), shape(16, 256)],
        [keep, came, early_keep, early_came],
    )
    one = send(total, to_own_group(1))
    three = send(total, to_own_group(3))
    two = send(pay, to_group(2))
    kred, mred = call(last_kernel, [shape(64, 256), shape(16, 256)], [base, mass_base, one, two, three])
    return (kred.T[None], mred.T[None])


def solution(mesh):
    in_specs = (
        P("leaf", "rows", None),
        P("leaf", "rows", None),
        P("leaf", "rows", None),
        P("leaf", "rows", None),
        P("leaf", "rows", None),
        P("leaf", "rows"),
        P("leaf", "rows"),
    )
    out_specs = (P("leaf", None, "rows"), P("leaf", None, "rows"))
    return jax.shard_map(shards, mesh=mesh, in_specs=in_specs, out_specs=out_specs, check_vma=False)
```

```python
import functools

import jax
import jax.numpy as jnp
from jax import lax
from jax.experimental import pallas as pl
from jax.experimental.pallas import tpu as pltpu
from jax.sharding import PartitionSpec as P

F32, BF16 = jnp.float32, jnp.bfloat16
BLK = 64
MIB = 2**20
COUPLE, SHIFT, MASS, KCOLS, LINKS, AUX = 0, 1024, 1032, 1040, 1056, 1072
VMEM = pl.BlockSpec(memory_space=pltpu.VMEM)
SMEM = pl.BlockSpec(memory_space=pltpu.SMEM)
ANY = pl.BlockSpec(memory_space=pl.ANY)
HBM = pl.BlockSpec(memory_space=pltpu.HBM)


def place():
    row = lax.axis_index("rows")
    return row // 4, (row // 2) % 2, row % 2


def send(value, to):
    leaves, rows = lax.axis_size("leaf"), lax.axis_size("rows")
    pairs = []
    for leaf in range(leaves):
        for row in range(rows):
            target = to(leaf, row)
            if target is not None:
                pairs.append((leaf * rows + row, target[0] * rows + target[1]))
    return lax.ppermute(value, ("leaf", "rows"), pairs)


def to_core(leaf, row):
    return leaf, row ^ 1


def to_side(leaf, row):
    return leaf, row ^ 2


def ring(forward):
    def to(leaf, row):
        step = 2 if (row % 2 == 0) == forward else -2
        return leaf, (row + step) % 16

    return to


def to_group(mask):
    return lambda leaf, row: (leaf, row ^ (4 * mask))


def to_own_group(mask):
    def to(leaf, row):
        return (leaf, 4 * (leaf % 4) + row % 4) if row // 4 == (leaf % 4) ^ mask else None

    return to


def call(body, outs, arrays, far=(), scratch=(), flops=0, vmem=8, aliases=None):
    moved = sum(x.size * x.dtype.itemsize for x in [*arrays, *far, *outs])
    return pl.pallas_call(
        body,
        out_shape=outs,
        in_specs=[VMEM] * len(arrays) + [HBM] * len(far),
        out_specs=[VMEM] * len(outs),
        scratch_shapes=list(scratch),
        input_output_aliases=aliases or {},
        compiler_params=pltpu.CompilerParams(vmem_limit_bytes=vmem * MIB),
        cost_estimate=pl.CostEstimate(flops=flops, bytes_accessed=moved, transcendentals=0),
    )(*arrays, *far)


def fetch(pairs, sems):
    copies = [pltpu.make_async_copy(src, dst, sems.at[n]) for n, (src, dst) in enumerate(pairs)]
    for copy in copies:
        copy.start()
    return copies


def shape(*dims, dtype=F32):
    return jax.ShapeDtypeStruct(dims, dtype)


def mine_of(width, column):
    here = lax.broadcasted_iota(jnp.int32, (width, 128), 0)
    want = column(lax.broadcasted_iota(jnp.int32, (width, 128), 1))
    return (here == want).astype(F32).astype(BF16)


def dot(a, b):
    return jnp.dot(a, b, preferred_element_type=F32)


def dot_t(a, b):
    return lax.dot_general(a, b, (((0,), (0,)), ((), ())), preferred_element_type=F32)


def after(value, *others):
    return lax.optimization_barrier((value, *others))[0]


def aux_kernel(couple_at, kcols_at, links_at, shift_at, mass_at, out, couple, kcols, links, shift, mass, sems):
    held = (couple, kcols, links, shift, mass)
    for copy in fetch(zip((couple_at, kcols_at, links_at, shift_at, mass_at), held), sems):
        copy.wait()
    out[COUPLE : COUPLE + 1024, :] = couple[0].astype(F32)
    for k in range(8):
        out[SHIFT + k : SHIFT + k + 1, :] = shift[:, k * 128 : (k + 1) * 128]
        out[MASS + k : MASS + k + 1, :] = mass[:, k * 128 : (k + 1) * 128]
    out[KCOLS:AUX, :] = jnp.zeros((AUX - KCOLS, 128), F32)
    out[KCOLS : KCOLS + 16, 0:26] = kcols[0].astype(F32)
    out[LINKS : LINKS + 2, 0:16] = links[0].astype(F32)


def mine(core):
    return mine_of(256, lambda n: 64 * core + n + jnp.where(n >= 64, 64, 0))


def first_kernel(own, held, half):
    _, _, core = place()
    held[...] = own[...]
    half[...] = dot(own[...], mine(core)).astype(BF16)


def half_kernel(own, own_half, other, out, both):
    _, _, core = place()
    out[pl.ds(pl.multiple_of(core * 1024, 1024), 1024), :] = own_half[...]
    out[pl.ds(pl.multiple_of((1 - core) * 1024, 1024), 1024), :] = dot(other[...], mine(core)).astype(BF16)
    both[0:1024, :] = own[...]
    both[1024:2048, :] = other[...]


def spread(dst, rows_own, rows_other):
    for part, rows in enumerate((rows_own, rows_other)):
        turned = jnp.transpose(jnp.concatenate([rows, jnp.zeros((120, 128), F32)], axis=0))
        for k in range(8):
            dst[part * 1024 + k * 128 : part * 1024 + (k + 1) * 128, :] = jnp.broadcast_to(
                turned[:, k : k + 1], (128, 128)
            )


def early_kernel(both, aux, aux_other, partner, to_send, to_keep, mred, coupled, weights, masked, spots, at, sem):
    _, _, core = place()
    spots[...] = jnp.zeros((8, 128), jnp.int32)
    for part, rows in enumerate((aux, aux_other)):
        links = rows[LINKS : LINKS + 2, 0:16].astype(jnp.int32)
        spots[part : part + 1, 0:16] = part * 1024 + jnp.where(core == 0, links[0:1, :], links[1:2, :]) * BLK
    copy = pltpu.make_async_copy(spots, at, sem)
    copy.start()
    mine = lax.broadcasted_iota(jnp.int32, (1024, 128), 1) // BLK == core
    for part, rows in enumerate((aux, aux_other)):
        couple = rows[COUPLE : COUPLE + 1024, :]
        masked[part * 1024 : (part + 1) * 1024, :] = jnp.where(mine, couple, 0.0).astype(BF16)
    copy.wait()

    def one(b, carry):
        rows = pl.ds(pl.multiple_of(b * BLK, BLK), BLK)
        block = partner[pl.ds(pl.multiple_of(at[b // 16, b % 16], BLK), BLK), :]
        coupled[rows, :] = dot(masked[rows, :], jnp.concatenate([block, block], axis=0)).astype(BF16)
        return carry

    lax.fori_loop(0, 32, one, 0, unroll=8)
    spread(weights, aux[MASS : MASS + 8, :], aux_other[MASS : MASS + 8, :])
    pick = mine_of(256, lambda n: 64 * ((n % 64) // 16) + 32 * (n // 64) + 16 * core + n % 16)
    weighted = (weights[...] * dot(both[...], pick)).astype(BF16)
    mred[...] = dot_t(weighted, both[...])
    term = dot_t(coupled[...], both[...])
    for k in range(2):
        low, high = term[k * 128 : k * 128 + 64, :], term[k * 128 + 64 : k * 128 + 128, :]
        to_keep[k * 64 : (k + 1) * 64, :] = jnp.where(core == 0, low, high)
        to_send[k * 64 : (k + 1) * 64, :] = jnp.where(core == 0, high, low)


def turn_kernel(kept, came, mred, to_send, to_keep):
    _, side, core = place()
    sib = jnp.where(core == 0, kept[...], came[...])
    cous = jnp.where(core == 0, came[...], kept[...])
    for t, term in enumerate((sib, cous, mred[...])):
        low, high = term[0:64, :], term[64:128, :]
        to_send[t * 64 : (t + 1) * 64, :] = jnp.where(side == 0, high, low)
        to_keep[t * 64 : (t + 1) * 64, :] = jnp.where(side == 0, low, high)


def split_kernel(kept, came, to_send, to_keep):
    group, _, _ = place()
    odd = (group ^ (lax.axis_index("leaf") % 4)) % 2 == 1
    sib = kept[0:64, :] + came[0:64, :]
    cous = kept[64:128, :] + came[64:128, :]
    mass = kept[128:192, :] + came[128:192, :]
    to_keep[0:64, :] = jnp.where(odd, sib, cous)
    to_send[0:64, :] = jnp.where(odd, cous, sib)
    low = group % 2 == 0
    for k in range(2):
        even, uneven = mass[k * 32 : k * 32 + 16, :], mass[k * 32 + 16 : k * 32 + 32, :]
        to_keep[64 + k * 16 : 80 + k * 16, :] = jnp.where(low, even, uneven)
        to_send[64 + k * 16 : 80 + k * 16, :] = jnp.where(low, uneven, even)


def stage_kernel(both, aux, aux_other, *refs):
    kcols_at, stiff, stiff_other = refs[:3]
    pieces = refs[3:10]
    table, matrix, start, spots, kcols, sems = refs[10:]
    _, _, core = place()
    chip = lax.axis_index("rows") // 2
    places = [2048 * d for d in (0, 7, 1, 6, 2, 5, 3)]
    pairs = [(kcols_at, kcols), (pieces[0], table.at[0:2048, :])]
    pairs += [(piece, table.at[lo : lo + 2048, :]) for piece, lo in list(zip(pieces, places))[1:]]
    pairs += [(stiff.at[0], matrix.at[0:1024, :]), (stiff_other, matrix.at[1024:2048, :])]
    copies = fetch(pairs, sems)
    spread(start, aux[SHIFT : SHIFT + 8, :], aux_other[SHIFT : SHIFT + 8, :])
    copies[0].wait()
    copies[1].wait()
    spots[...] = jnp.zeros((32, 128), jnp.int32)
    for part in range(2):
        column = kcols[0] if part == 0 else aux_other[KCOLS : KCOLS + 16, 0:26].astype(jnp.int32)
        ahead = column // 32 - chip
        ahead = jnp.where(core == 0, ahead, -ahead) & 7
        spots[part * 16 : (part + 1) * 16, 0:26] = ahead * 2048 + (column % 32) * BLK
    for part in range(2):
        rows = slice(part * 1024, (part + 1) * 1024)
        mine = pl.ds(pl.multiple_of((part * 1024 + core * 1024) % 2048, 1024), 1024)
        start[rows, :] = start[rows, :] * table[mine, :].astype(F32)
    for copy in copies[2:]:
        copy.wait()


def own_kernel(table, matrix, start, spots, both, last_at, to_send, to_keep, full, image, at, sems):
    _, side, _ = place()
    copies = fetch([(spots, at), (last_at, full.at[4 * 2048 : 5 * 2048, :])], sems)
    for copy in copies:
        copy.wait()

    def one(b, carry):
        rows = pl.ds(pl.multiple_of(b * BLK, BLK), BLK)
        total = start[rows, :]
        blocks = [full[pl.ds(pl.multiple_of(at[b, k], BLK), BLK), :] for k in range(26)]
        for g in range(0, 26, 4):
            picked = jnp.concatenate(blocks[g : g + 4], axis=0)
            width = picked.shape[0]
            total += dot(matrix[rows, g * BLK : g * BLK + width], picked)
        image[rows, :] = total.astype(BF16)
        return carry

    lax.fori_loop(0, 32, one, 0, unroll=8)
    result = dot_t(image[...], both[...])
    low, high = result[0:64, :], result[64:128, :]
    to_send[...] = jnp.where(side == 0, high, low)
    to_keep[...] = jnp.where(side == 0, low, high)


def gather_kernel(kept, came, early_kept, early_came, total, pay, base, mass_base):
    group, _, _ = place()
    term = group ^ (lax.axis_index("leaf") % 4)
    own = kept[...] + came[...]
    early = early_kept[0:64, :] + early_came[0:64, :]
    total[...] = own
    zero = jnp.zeros_like(own)
    pay[0:64, :] = jnp.where(term == 2, own, jnp.where(term == 1, zero, early))
    base[...] = jnp.where(term == 0, own, jnp.where(term == 3, zero, early))
    first = early_kept[64:80, :] + early_came[64:80, :]
    second = early_kept[80:96, :] + early_came[80:96, :]
    low = group < 2
    pay[64:80, :] = jnp.where(low, second, first)
    mass_base[...] = jnp.where(low, first, second)


def last_kernel(base, mass_base, one, two, three, kred, mred):
    kred[...] = base[...] + one[...] + two[0:64, :] + three[...]
    mred[...] = mass_base[...] + two[64:80, :]


def shards(basis, stiff, kcols, couple, links, shift, mass):
    own = basis[0]
    links = links.transpose(0, 2, 1)
    other = send(own, to_core)
    own_held, own_half = call(first_kernel, [shape(1024, 256, dtype=BF16), shape(1024, 128, dtype=BF16)], [own])
    half, both = call(
        half_kernel,
        [shape(2048, 128, dtype=BF16), shape(2048, 256, dtype=BF16)],
        [own_held, own_half, other],
        flops=4 * 10**10,
    )
    left1 = send(half, ring(True))
    (aux,) = call(
        aux_kernel,
        [shape(AUX, 128)],
        [],
        [couple, after(kcols, own_held), links, shift, mass],
        [
            pltpu.VMEM((1, 1024, 128), BF16),
            pltpu.VMEM((1, 16, 26), jnp.int32),
            pltpu.VMEM((1, 2, 16), jnp.int32),
            pltpu.VMEM((1, 1024), F32),
            pltpu.VMEM((1, 1024), F32),
            pltpu.SemaphoreType.DMA((5,)),
        ],
        vmem=56,
    )
    right1 = send(half, ring(False))
    partner = send(both, lambda leaf, row: (leaf ^ (1 + row % 2), row))
    stiff_other = send(stiff[0], to_core)
    aux_other = send(after(aux, stiff_other), to_core)
    left2, right2 = send(left1, ring(True)), send(right1, ring(False))
    go, keep, mass_part = call(
        early_kernel,
        [shape(128, 256)] * 3,
        [both, aux, aux_other, partner],
        [],
        [
            pltpu.VMEM((2048, 256), BF16),
            pltpu.VMEM((2048, 128), F32),
            pltpu.VMEM((2048, 128), BF16),
            pltpu.VMEM((8, 128), jnp.int32),
            pltpu.SMEM((8, 128), jnp.int32),
            pltpu.SemaphoreType.DMA,
        ],
        flops=2**30,
        vmem=16,
    )
    came = send(go, to_core)
    go, keep = call(turn_kernel, [shape(192, 256)] * 2, [keep, came, mass_part])
    left3, right3 = send(left2, ring(True)), send(after(right2, go), ring(False))
    left4 = send(left3, ring(True))
    came = send(go, to_side)
    go, early_keep = call(split_kernel, [shape(96, 256)] * 2, [keep, came], flops=5 * 10**9)
    early_came = send(go, to_group(1))

    table, matrix, start, spots = call(
        stage_kernel,
        [shape(16384, 128, dtype=BF16), shape(2048, 1664, dtype=BF16), shape(2048, 128), shape(32, 128, dtype=jnp.int32)],
        [both, aux, aux_other],
        [kcols, stiff, stiff_other, half, left1, right1, left2, right2, left3, right3],
        [pltpu.VMEM((1, 16, 26), jnp.int32), pltpu.SemaphoreType.DMA((10,))],
    )
    go, keep, _ = call(
        own_kernel,
        [shape(64, 256), shape(64, 256), shape(16384, 128, dtype=BF16)],
        [table, matrix, start, spots, both],
        [left4],
        [pltpu.VMEM((2048, 128), BF16), pltpu.SMEM((32, 128), jnp.int32), pltpu.SemaphoreType.DMA((2,))],
        flops=2**30,
        aliases={0: 2},
    )
    came = send(go, to_side)
    total, pay, base, mass_base = call(
        gather_kernel,
        [shape(64, 256), shape(80, 256), shape(64, 256), shape(16, 256)],
        [keep, came, early_keep, early_came],
    )
    one = send(total, to_own_group(1))
    three = send(total, to_own_group(3))
    two = send(pay, to_group(2))
    kred, mred = call(last_kernel, [shape(64, 256), shape(16, 256)], [base, mass_base, one, two, three])
    return (kred.T[None], mred.T[None])


def solution(mesh):
    in_specs = (
        P("leaf", "rows", None),
        P("leaf", "rows", None),
        P("leaf", "rows", None),
        P("leaf", "rows", None),
        P("leaf", "rows", None),
        P("leaf", "rows"),
        P("leaf", "rows"),
    )
    out_specs = (P("leaf", None, "rows"), P("leaf", None, "rows"))
    return jax.shard_map(shards, mesh=mesh, in_specs=in_specs, out_specs=out_specs, check_vma=False)
```

```python
import functools

import jax
import jax.numpy as jnp
from jax import lax
from jax.experimental import pallas as pl
from jax.experimental.pallas import tpu as pltpu
from jax.sharding import PartitionSpec as P

F32, BF16 = jnp.float32, jnp.bfloat16
BLK = 64
MIB = 2**20
COUPLE, SHIFT, MASS, KCOLS, LINKS, AUX = 0, 1024, 1032, 1040, 1056, 1072
VMEM = pl.BlockSpec(memory_space=pltpu.VMEM)
SMEM = pl.BlockSpec(memory_space=pltpu.SMEM)
ANY = pl.BlockSpec(memory_space=pl.ANY)
HBM = pl.BlockSpec(memory_space=pltpu.HBM)


def place():
    row = lax.axis_index("rows")
    return row // 4, (row // 2) % 2, row % 2


def send(value, to):
    leaves, rows = lax.axis_size("leaf"), lax.axis_size("rows")
    pairs = []
    for leaf in range(leaves):
        for row in range(rows):
            target = to(leaf, row)
            if target is not None:
                pairs.append((leaf * rows + row, target[0] * rows + target[1]))
    return lax.ppermute(value, ("leaf", "rows"), pairs)


def to_core(leaf, row):
    return leaf, row ^ 1


def to_side(leaf, row):
    return leaf, row ^ 2


def ring(forward):
    def to(leaf, row):
        step = 2 if (row % 2 == 0) == forward else -2
        return leaf, (row + step) % 16

    return to


def to_group(mask):
    return lambda leaf, row: (leaf, row ^ (4 * mask))


def to_own_group(mask):
    def to(leaf, row):
        return (leaf, 4 * (leaf % 4) + row % 4) if row // 4 == (leaf % 4) ^ mask else None

    return to


def call(body, outs, arrays, far=(), scratch=(), flops=0, vmem=8, aliases=None):
    moved = sum(x.size * x.dtype.itemsize for x in [*arrays, *far, *outs])
    return pl.pallas_call(
        body,
        out_shape=outs,
        in_specs=[VMEM] * len(arrays) + [HBM] * len(far),
        out_specs=[VMEM] * len(outs),
        scratch_shapes=list(scratch),
        input_output_aliases=aliases or {},
        compiler_params=pltpu.CompilerParams(vmem_limit_bytes=vmem * MIB),
        cost_estimate=pl.CostEstimate(flops=flops, bytes_accessed=moved, transcendentals=0),
    )(*arrays, *far)


def fetch(pairs, sems):
    copies = [pltpu.make_async_copy(src, dst, sems.at[n]) for n, (src, dst) in enumerate(pairs)]
    for copy in copies:
        copy.start()
    return copies


def shape(*dims, dtype=F32):
    return jax.ShapeDtypeStruct(dims, dtype)


def mine_of(width, column):
    here = lax.broadcasted_iota(jnp.int32, (width, 128), 0)
    want = column(lax.broadcasted_iota(jnp.int32, (width, 128), 1))
    return (here == want).astype(F32).astype(BF16)


def dot(a, b):
    return jnp.dot(a, b, preferred_element_type=F32)


def dot_t(a, b):
    return lax.dot_general(a, b, (((0,), (0,)), ((), ())), preferred_element_type=F32)


def after(value, *others):
    return lax.optimization_barrier((value, *others))[0]


def aux_kernel(couple_at, kcols_at, links_at, shift_at, mass_at, out, couple, kcols, links, shift, mass, sems):
    held = (couple, kcols, links, shift, mass)
    for copy in fetch(zip((couple_at, kcols_at, links_at, shift_at, mass_at), held), sems):
        copy.wait()
    out[COUPLE : COUPLE + 1024, :] = couple[0].astype(F32)
    for k in range(8):
        out[SHIFT + k : SHIFT + k + 1, :] = shift[:, k * 128 : (k + 1) * 128]
        out[MASS + k : MASS + k + 1, :] = mass[:, k * 128 : (k + 1) * 128]
    out[KCOLS:AUX, :] = jnp.zeros((AUX - KCOLS, 128), F32)
    out[KCOLS : KCOLS + 16, 0:26] = kcols[0].astype(F32)
    out[LINKS : LINKS + 2, 0:16] = links[0].astype(F32)


def mine(core):
    return mine_of(256, lambda n: 64 * core + n + jnp.where(n >= 64, 64, 0))


def first_kernel(own, held, half):
    _, _, core = place()
    held[...] = own[...]
    half[...] = dot(own[...], mine(core)).astype(BF16)


def half_kernel(own, own_half, other, out, both):
    _, _, core = place()
    out[pl.ds(pl.multiple_of(core * 1024, 1024), 1024), :] = own_half[...]
    out[pl.ds(pl.multiple_of((1 - core) * 1024, 1024), 1024), :] = dot(other[...], mine(core)).astype(BF16)
    both[0:1024, :] = own[...]
    both[1024:2048, :] = other[...]


def spread(dst, rows_own, rows_other):
    for part, rows in enumerate((rows_own, rows_other)):
        turned = jnp.transpose(jnp.concatenate([rows, jnp.zeros((120, 128), F32)], axis=0))
        for k in range(8):
            dst[part * 1024 + k * 128 : part * 1024 + (k + 1) * 128, :] = jnp.broadcast_to(
                turned[:, k : k + 1], (128, 128)
            )


def mass_kernel(both, aux, aux_other, mred, weights):
    _, _, core = place()
    spread(weights, aux[MASS : MASS + 8, :], aux_other[MASS : MASS + 8, :])
    pick = mine_of(256, lambda n: 64 * ((n % 64) // 16) + 32 * (n // 64) + 16 * core + n % 16)
    weighted = (weights[...] * dot(both[...], pick)).astype(BF16)
    mred[...] = dot_t(weighted, both[...])


def early_kernel(both, aux, aux_other, partner, to_send, to_keep, coupled, masked, spots, at, sem):
    _, _, core = place()
    spots[...] = jnp.zeros((8, 128), jnp.int32)
    for part, rows in enumerate((aux, aux_other)):
        links = rows[LINKS : LINKS + 2, 0:16].astype(jnp.int32)
        spots[part : part + 1, 0:16] = part * 1024 + jnp.where(core == 0, links[0:1, :], links[1:2, :]) * BLK
    copy = pltpu.make_async_copy(spots, at, sem)
    copy.start()
    mine = lax.broadcasted_iota(jnp.int32, (1024, 128), 1) // BLK == core
    for part, rows in enumerate((aux, aux_other)):
        couple = rows[COUPLE : COUPLE + 1024, :]
        masked[part * 1024 : (part + 1) * 1024, :] = jnp.where(mine, couple, 0.0).astype(BF16)
    copy.wait()

    def one(b, carry):
        rows = pl.ds(pl.multiple_of(b * BLK, BLK), BLK)
        block = partner[pl.ds(pl.multiple_of(at[b // 16, b % 16], BLK), BLK), :]
        coupled[rows, :] = dot(masked[rows, :], jnp.concatenate([block, block], axis=0)).astype(BF16)
        return carry

    lax.fori_loop(0, 32, one, 0, unroll=16)
    term = dot_t(coupled[...], both[...])
    for k in range(2):
        low, high = term[k * 128 : k * 128 + 64, :], term[k * 128 + 64 : k * 128 + 128, :]
        to_keep[k * 64 : (k + 1) * 64, :] = jnp.where(core == 0, low, high)
        to_send[k * 64 : (k + 1) * 64, :] = jnp.where(core == 0, high, low)


def turn_kernel(kept, came, mred, to_send, to_keep):
    _, side, core = place()
    sib = jnp.where(core == 0, kept[...], came[...])
    cous = jnp.where(core == 0, came[...], kept[...])
    for t, term in enumerate((sib, cous, mred[...])):
        low, high = term[0:64, :], term[64:128, :]
        to_send[t * 64 : (t + 1) * 64, :] = jnp.where(side == 0, high, low)
        to_keep[t * 64 : (t + 1) * 64, :] = jnp.where(side == 0, low, high)


def split_kernel(kept, came, to_send, to_keep):
    group, _, _ = place()
    odd = (group ^ (lax.axis_index("leaf") % 4)) % 2 == 1
    sib = kept[0:64, :] + came[0:64, :]
    cous = kept[64:128, :] + came[64:128, :]
    mass = kept[128:192, :] + came[128:192, :]
    to_keep[0:64, :] = jnp.where(odd, sib, cous)
    to_send[0:64, :] = jnp.where(odd, cous, sib)
    low = group % 2 == 0
    for k in range(2):
        even, uneven = mass[k * 32 : k * 32 + 16, :], mass[k * 32 + 16 : k * 32 + 32, :]
        to_keep[64 + k * 16 : 80 + k * 16, :] = jnp.where(low, even, uneven)
        to_send[64 + k * 16 : 80 + k * 16, :] = jnp.where(low, uneven, even)


def stage_kernel(both, aux, aux_other, *refs):
    kcols_at, stiff, stiff_other = refs[:3]
    pieces = refs[3:10]
    table, matrix, start, spots, kcols, sems = refs[10:]
    _, _, core = place()
    chip = lax.axis_index("rows") // 2
    places = [2048 * d for d in (0, 7, 1, 6, 2, 5, 3)]
    pairs = [(kcols_at, kcols), (pieces[0], table.at[0:2048, :])]
    pairs += [(piece, table.at[lo : lo + 2048, :]) for piece, lo in list(zip(pieces, places))[1:]]
    pairs += [(stiff.at[0], matrix.at[0:1024, :]), (stiff_other, matrix.at[1024:2048, :])]
    copies = fetch(pairs, sems)
    spread(start, aux[SHIFT : SHIFT + 8, :], aux_other[SHIFT : SHIFT + 8, :])
    copies[0].wait()
    copies[1].wait()
    spots[...] = jnp.zeros((32, 128), jnp.int32)
    for part in range(2):
        column = kcols[0] if part == 0 else aux_other[KCOLS : KCOLS + 16, 0:26].astype(jnp.int32)
        ahead = column // 32 - chip
        ahead = jnp.where(core == 0, ahead, -ahead) & 7
        spots[part * 16 : (part + 1) * 16, 0:26] = ahead * 2048 + (column % 32) * BLK
    for part in range(2):
        rows = slice(part * 1024, (part + 1) * 1024)
        mine = pl.ds(pl.multiple_of((part * 1024 + core * 1024) % 2048, 1024), 1024)
        start[rows, :] = start[rows, :] * table[mine, :].astype(F32)
    for copy in copies[2:]:
        copy.wait()


def own_kernel(table, matrix, start, spots, both, last_at, to_send, to_keep, full, image, at, sems):
    _, side, _ = place()
    copies = fetch([(spots, at), (last_at, full.at[4 * 2048 : 5 * 2048, :])], sems)
    for copy in copies:
        copy.wait()

    def one(b, carry):
        rows = pl.ds(pl.multiple_of(b * BLK, BLK), BLK)
        total = start[rows, :]
        blocks = [full[pl.ds(pl.multiple_of(at[b, k], BLK), BLK), :] for k in range(26)]
        for g in range(0, 26, 4):
            picked = jnp.concatenate(blocks[g : g + 4], axis=0)
            width = picked.shape[0]
            total += dot(matrix[rows, g * BLK : g * BLK + width], picked)
        image[rows, :] = total.astype(BF16)
        return carry

    lax.fori_loop(0, 32, one, 0, unroll=16)
    result = dot_t(image[...], both[...])
    low, high = result[0:64, :], result[64:128, :]
    to_send[...] = jnp.where(side == 0, high, low)
    to_keep[...] = jnp.where(side == 0, low, high)


def gather_kernel(kept, came, early_kept, early_came, total, pay, base, mass_base):
    group, _, _ = place()
    term = group ^ (lax.axis_index("leaf") % 4)
    own = kept[...] + came[...]
    early = early_kept[0:64, :] + early_came[0:64, :]
    total[...] = own
    zero = jnp.zeros_like(own)
    pay[0:64, :] = jnp.where(term == 2, own, jnp.where(term == 1, zero, early))
    base[...] = jnp.where(term == 0, own, jnp.where(term == 3, zero, early))
    first = early_kept[64:80, :] + early_came[64:80, :]
    second = early_kept[80:96, :] + early_came[80:96, :]
    low = group < 2
    pay[64:80, :] = jnp.where(low, second, first)
    mass_base[...] = jnp.where(low, first, second)


def last_kernel(base, mass_base, one, two, three, kred, mred):
    kred[...] = base[...] + one[...] + two[0:64, :] + three[...]
    mred[...] = mass_base[...] + two[64:80, :]


def shards(basis, stiff, kcols, couple, links, shift, mass):
    own = basis[0]
    links = links.transpose(0, 2, 1)
    other = send(own, to_core)
    own_held, own_half = call(first_kernel, [shape(1024, 256, dtype=BF16), shape(1024, 128, dtype=BF16)], [own])
    half, both = call(
        half_kernel,
        [shape(2048, 128, dtype=BF16), shape(2048, 256, dtype=BF16)],
        [own_held, own_half, other],
        flops=4 * 10**10,
    )
    left1 = send(half, ring(True))
    (aux,) = call(
        aux_kernel,
        [shape(AUX, 128)],
        [],
        [couple, after(kcols, own_held), links, shift, mass],
        [
            pltpu.VMEM((1, 1024, 128), BF16),
            pltpu.VMEM((1, 16, 26), jnp.int32),
            pltpu.VMEM((1, 2, 16), jnp.int32),
            pltpu.VMEM((1, 1024), F32),
            pltpu.VMEM((1, 1024), F32),
            pltpu.SemaphoreType.DMA((5,)),
        ],
        vmem=56,
    )
    right1 = send(half, ring(False))
    partner = send(both, lambda leaf, row: (leaf ^ (1 + row % 2), row))
    stiff_other = send(stiff[0], to_core)
    aux_other = send(after(aux, stiff_other), to_core)
    (mass_part,) = call(
        mass_kernel, [shape(128, 256)], [both, aux, aux_other], [], [pltpu.VMEM((2048, 128), F32)], 0
    )
    left2, right2 = send(left1, ring(True)), send(right1, ring(False))
    go, keep = call(
        early_kernel,
        [shape(128, 256)] * 2,
        [both, aux, aux_other, partner],
        [],
        [
            pltpu.VMEM((2048, 256), BF16),
            pltpu.VMEM((2048, 128), BF16),
            pltpu.VMEM((8, 128), jnp.int32),
            pltpu.SMEM((8, 128), jnp.int32),
            pltpu.SemaphoreType.DMA,
        ],
        flops=2**30,
        vmem=16,
    )
    came = send(go, to_core)
    go, keep = call(turn_kernel, [shape(192, 256)] * 2, [keep, came, mass_part])
    left3, right3 = send(left2, ring(True)), send(after(right2, go), ring(False))
    left4 = send(left3, ring(True))
    came = send(go, to_side)
    go, early_keep = call(split_kernel, [shape(96, 256)] * 2, [keep, came], flops=5 * 10**9)
    early_came = send(go, to_group(1))

    table, matrix, start, spots = call(
        stage_kernel,
        [shape(16384, 128, dtype=BF16), shape(2048, 1664, dtype=BF16), shape(2048, 128), shape(32, 128, dtype=jnp.int32)],
        [both, aux, aux_other],
        [kcols, stiff, stiff_other, half, left1, right1, left2, right2, left3, right3],
        [pltpu.VMEM((1, 16, 26), jnp.int32), pltpu.SemaphoreType.DMA((10,))],
    )
    go, keep, _ = call(
        own_kernel,
        [shape(64, 256), shape(64, 256), shape(16384, 128, dtype=BF16)],
        [table, matrix, start, spots, both],
        [left4],
        [pltpu.VMEM((2048, 128), BF16), pltpu.SMEM((32, 128), jnp.int32), pltpu.SemaphoreType.DMA((2,))],
        flops=2**30,
        aliases={0: 2},
    )
    came = send(go, to_side)
    total, pay, base, mass_base = call(
        gather_kernel,
        [shape(64, 256), shape(80, 256), shape(64, 256), shape(16, 256)],
        [keep, came, early_keep, early_came],
    )
    one = send(total, to_own_group(1))
    three = send(total, to_own_group(3))
    two = send(pay, to_group(2))
    kred, mred = call(last_kernel, [shape(64, 256), shape(16, 256)], [base, mass_base, one, two, three])
    return (kred.T[None], mred.T[None])


def solution(mesh):
    in_specs = (
        P("leaf", "rows", None),
        P("leaf", "rows", None),
        P("leaf", "rows", None),
        P("leaf", "rows", None),
        P("leaf", "rows", None),
        P("leaf", "rows"),
        P("leaf", "rows"),
    )
    out_specs = (P("leaf", None, "rows"), P("leaf", None, "rows"))
    return jax.shard_map(shards, mesh=mesh, in_specs=in_specs, out_specs=out_specs, check_vma=False)
```

```python
import functools

import jax
import jax.numpy as jnp
from jax import lax
from jax.experimental import pallas as pl
from jax.experimental.pallas import tpu as pltpu
from jax.sharding import PartitionSpec as P

F32, BF16 = jnp.float32, jnp.bfloat16
BLK = 64
MIB = 2**20
COUPLE, SHIFT, MASS, KCOLS, LINKS, AUX = 0, 1024, 1032, 1040, 1056, 1072
VMEM = pl.BlockSpec(memory_space=pltpu.VMEM)
SMEM = pl.BlockSpec(memory_space=pltpu.SMEM)
ANY = pl.BlockSpec(memory_space=pl.ANY)
HBM = pl.BlockSpec(memory_space=pltpu.HBM)


def place():
    row = lax.axis_index("rows")
    return row // 4, (row // 2) % 2, row % 2


def send(value, to):
    leaves, rows = lax.axis_size("leaf"), lax.axis_size("rows")
    pairs = []
    for leaf in range(leaves):
        for row in range(rows):
            target = to(leaf, row)
            if target is not None:
                pairs.append((leaf * rows + row, target[0] * rows + target[1]))
    return lax.ppermute(value, ("leaf", "rows"), pairs)


def to_core(leaf, row):
    return leaf, row ^ 1


def to_side(leaf, row):
    return leaf, row ^ 2


def ring(forward):
    def to(leaf, row):
        step = 2 if (row % 2 == 0) == forward else -2
        return leaf, (row + step) % 16

    return to


def to_group(mask):
    return lambda leaf, row: (leaf, row ^ (4 * mask))


def to_own_group(mask):
    def to(leaf, row):
        return (leaf, 4 * (leaf % 4) + row % 4) if row // 4 == (leaf % 4) ^ mask else None

    return to


def call(body, outs, arrays, far=(), scratch=(), flops=0, vmem=8, aliases=None):
    moved = sum(x.size * x.dtype.itemsize for x in [*arrays, *far, *outs])
    return pl.pallas_call(
        body,
        out_shape=outs,
        in_specs=[VMEM] * len(arrays) + [HBM] * len(far),
        out_specs=[VMEM] * len(outs),
        scratch_shapes=list(scratch),
        input_output_aliases=aliases or {},
        compiler_params=pltpu.CompilerParams(vmem_limit_bytes=vmem * MIB),
        cost_estimate=pl.CostEstimate(flops=flops, bytes_accessed=moved, transcendentals=0),
    )(*arrays, *far)


def fetch(pairs, sems):
    copies = [pltpu.make_async_copy(src, dst, sems.at[n]) for n, (src, dst) in enumerate(pairs)]
    for copy in copies:
        copy.start()
    return copies


def shape(*dims, dtype=F32):
    return jax.ShapeDtypeStruct(dims, dtype)


def mine_of(width, column):
    here = lax.broadcasted_iota(jnp.int32, (width, 128), 0)
    want = column(lax.broadcasted_iota(jnp.int32, (width, 128), 1))
    return (here == want).astype(F32).astype(BF16)


def dot(a, b):
    return jnp.dot(a, b, preferred_element_type=F32)


def dot_t(a, b):
    return lax.dot_general(a, b, (((0,), (0,)), ((), ())), preferred_element_type=F32)


def after(value, *others):
    return lax.optimization_barrier((value, *others))[0]


def aux_kernel(couple_at, kcols_at, links_at, shift_at, mass_at, out, couple, kcols, links, shift, mass, sems):
    held = (couple, kcols, links, shift, mass)
    for copy in fetch(zip((couple_at, kcols_at, links_at, shift_at, mass_at), held), sems):
        copy.wait()
    out[COUPLE : COUPLE + 1024, :] = couple[0].astype(F32)
    for k in range(8):
        out[SHIFT + k : SHIFT + k + 1, :] = shift[:, k * 128 : (k + 1) * 128]
        out[MASS + k : MASS + k + 1, :] = mass[:, k * 128 : (k + 1) * 128]
    out[KCOLS:AUX, :] = jnp.zeros((AUX - KCOLS, 128), F32)
    out[KCOLS : KCOLS + 16, 0:26] = kcols[0].astype(F32)
    out[LINKS : LINKS + 2, 0:16] = links[0].astype(F32)


def mine(core):
    return mine_of(256, lambda n: 64 * core + n + jnp.where(n >= 64, 64, 0))


def first_kernel(own, held, half):
    _, _, core = place()
    held[...] = own[...]
    half[...] = dot(own[...], mine(core)).astype(BF16)


def half_kernel(own, own_half, other, out, both):
    _, _, core = place()
    out[pl.ds(pl.multiple_of(core * 1024, 1024), 1024), :] = own_half[...]
    out[pl.ds(pl.multiple_of((1 - core) * 1024, 1024), 1024), :] = dot(other[...], mine(core)).astype(BF16)
    both[0:1024, :] = own[...]
    both[1024:2048, :] = other[...]


def spread(dst, rows_own, rows_other):
    for part, rows in enumerate((rows_own, rows_other)):
        turned = jnp.transpose(jnp.concatenate([rows, jnp.zeros((120, 128), F32)], axis=0))
        for k in range(8):
            dst[part * 1024 + k * 128 : part * 1024 + (k + 1) * 128, :] = jnp.broadcast_to(
                turned[:, k : k + 1], (128, 128)
            )


def mass_kernel(both, aux, aux_other, mred, masked, spots, weights):
    _, _, core = place()
    spread(weights, aux[MASS : MASS + 8, :], aux_other[MASS : MASS + 8, :])
    pick = mine_of(256, lambda n: 64 * ((n % 64) // 16) + 32 * (n // 64) + 16 * core + n % 16)
    weighted = (weights[...] * dot(both[...], pick)).astype(BF16)
    mred[...] = dot_t(weighted, both[...])
    spots[...] = jnp.zeros((8, 128), jnp.int32)
    here = lax.broadcasted_iota(jnp.int32, (1024, 128), 1) // BLK == core
    for part, rows in enumerate((aux, aux_other)):
        links = rows[LINKS : LINKS + 2, 0:16].astype(jnp.int32)
        spots[part : part + 1, 0:16] = part * 1024 + jnp.where(core == 0, links[0:1, :], links[1:2, :]) * BLK
        couple = rows[COUPLE : COUPLE + 1024, :]
        masked[part * 1024 : (part + 1) * 1024, :] = jnp.where(here, couple, 0.0).astype(BF16)


def early_kernel(both, partner, mred, masked, spots, to_send, to_keep, coupled, at, sem):
    _, side, _ = place()
    copy = pltpu.make_async_copy(spots, at, sem)
    copy.start()
    copy.wait()

    def one(b, carry):
        rows = pl.ds(pl.multiple_of(b * BLK, BLK), BLK)
        block = partner[pl.ds(pl.multiple_of(at[b // 16, b % 16], BLK), BLK), :]
        coupled[rows, :] = dot(masked[rows, :], jnp.concatenate([block, block], axis=0)).astype(BF16)
        return carry

    lax.fori_loop(0, 32, one, 0, unroll=16)
    term = dot_t(coupled[...], both[...])
    for low, high, rows in (
        (term[0:128, :], term[128:256, :], slice(0, 128)),
        (mred[0:64, :], mred[64:128, :], slice(128, 192)),
    ):
        to_send[rows, :] = jnp.where(side == 0, high, low)
        to_keep[rows, :] = jnp.where(side == 0, low, high)


def turn_kernel(kept, came, to_send, to_keep):
    _, _, core = place()
    total = kept[...] + came[...]
    to_send[...] = jnp.where(core == 0, total[64:128, :], total[0:64, :])
    to_keep[0:64, :] = jnp.where(core == 0, total[0:64, :], total[64:128, :])
    to_keep[64:128, :] = total[128:192, :]


def split_kernel(kept, came, to_send, to_keep):
    group, _, core = place()
    odd = (group ^ (lax.axis_index("leaf") % 4)) % 2 == 1
    sib = jnp.where(core == 0, kept[0:64, :], came[...])
    cous = jnp.where(core == 0, came[...], kept[0:64, :])
    mass = kept[64:128, :]
    to_keep[0:64, :] = jnp.where(odd, sib, cous)
    to_send[0:64, :] = jnp.where(odd, cous, sib)
    low = group % 2 == 0
    for k in range(2):
        even, uneven = mass[k * 32 : k * 32 + 16, :], mass[k * 32 + 16 : k * 32 + 32, :]
        to_keep[64 + k * 16 : 80 + k * 16, :] = jnp.where(low, even, uneven)
        to_send[64 + k * 16 : 80 + k * 16, :] = jnp.where(low, uneven, even)


def stage_kernel(both, aux, aux_other, *refs):
    kcols_at, stiff, stiff_other = refs[:3]
    pieces = refs[3:10]
    table, matrix, start, spots, kcols, sems = refs[10:]
    _, _, core = place()
    chip = lax.axis_index("rows") // 2
    places = [2048 * d for d in (0, 7, 1, 6, 2, 5, 3)]
    pairs = [(kcols_at, kcols), (pieces[0], table.at[0:2048, :])]
    pairs += [(piece, table.at[lo : lo + 2048, :]) for piece, lo in list(zip(pieces, places))[1:]]
    pairs += [(stiff.at[0], matrix.at[0:1024, :]), (stiff_other, matrix.at[1024:2048, :])]
    copies = fetch(pairs, sems)
    spread(start, aux[SHIFT : SHIFT + 8, :], aux_other[SHIFT : SHIFT + 8, :])
    copies[0].wait()
    copies[1].wait()
    spots[...] = jnp.zeros((32, 128), jnp.int32)
    for part in range(2):
        column = kcols[0] if part == 0 else aux_other[KCOLS : KCOLS + 16, 0:26].astype(jnp.int32)
        ahead = column // 32 - chip
        ahead = jnp.where(core == 0, ahead, -ahead) & 7
        spots[part * 16 : (part + 1) * 16, 0:26] = ahead * 2048 + (column % 32) * BLK
    for part in range(2):
        rows = slice(part * 1024, (part + 1) * 1024)
        mine = pl.ds(pl.multiple_of((part * 1024 + core * 1024) % 2048, 1024), 1024)
        start[rows, :] = start[rows, :] * table[mine, :].astype(F32)
    for copy in copies[2:]:
        copy.wait()


def own_kernel(table, matrix, start, spots, both, last_at, to_send, to_keep, full, image, at, sems):
    _, side, _ = place()
    copies = fetch([(spots, at), (last_at, full.at[4 * 2048 : 5 * 2048, :])], sems)
    for copy in copies:
        copy.wait()

    def one(b, carry):
        rows = pl.ds(pl.multiple_of(b * BLK, BLK), BLK)
        total = start[rows, :]
        blocks = [full[pl.ds(pl.multiple_of(at[b, k], BLK), BLK), :] for k in range(26)]
        for g in range(0, 26, 4):
            picked = jnp.concatenate(blocks[g : g + 4], axis=0)
            width = picked.shape[0]
            total += dot(matrix[rows, g * BLK : g * BLK + width], picked)
        image[rows, :] = total.astype(BF16)
        return carry

    lax.fori_loop(0, 32, one, 0, unroll=16)
    result = dot_t(image[...], both[...])
    low, high = result[0:64, :], result[64:128, :]
    to_send[...] = jnp.where(side == 0, high, low)
    to_keep[...] = jnp.where(side == 0, low, high)


def gather_kernel(kept, came, early_kept, early_came, total, pay, base, mass_base):
    group, _, _ = place()
    term = group ^ (lax.axis_index("leaf") % 4)
    own = kept[...] + came[...]
    early = early_kept[0:64, :] + early_came[0:64, :]
    total[...] = own
    zero = jnp.zeros_like(own)
    pay[0:64, :] = jnp.where(term == 2, own, jnp.where(term == 1, zero, early))
    base[...] = jnp.where(term == 0, own, jnp.where(term == 3, zero, early))
    first = early_kept[64:80, :] + early_came[64:80, :]
    second = early_kept[80:96, :] + early_came[80:96, :]
    low = group < 2
    pay[64:80, :] = jnp.where(low, second, first)
    mass_base[...] = jnp.where(low, first, second)


def last_kernel(base, mass_base, one, two, three, kred, mred):
    kred[...] = base[...] + one[...] + two[0:64, :] + three[...]
    mred[...] = mass_base[...] + two[64:80, :]


def shards(basis, stiff, kcols, couple, links, shift, mass):
    own = basis[0]
    links = links.transpose(0, 2, 1)
    other = send(own, to_core)
    own_held, own_half = call(first_kernel, [shape(1024, 256, dtype=BF16), shape(1024, 128, dtype=BF16)], [own])
    half, both = call(
        half_kernel,
        [shape(2048, 128, dtype=BF16), shape(2048, 256, dtype=BF16)],
        [own_held, own_half, other],
        flops=4 * 10**10,
    )
    left1 = send(half, ring(True))
    (aux,) = call(
        aux_kernel,
        [shape(AUX, 128)],
        [],
        [couple, after(kcols, own_held), links, shift, mass],
        [
            pltpu.VMEM((1, 1024, 128), BF16),
            pltpu.VMEM((1, 16, 26), jnp.int32),
            pltpu.VMEM((1, 2, 16), jnp.int32),
            pltpu.VMEM((1, 1024), F32),
            pltpu.VMEM((1, 1024), F32),
            pltpu.SemaphoreType.DMA((5,)),
        ],
        vmem=56,
    )
    right1 = send(half, ring(False))
    partner = send(both, lambda leaf, row: (leaf ^ (1 + row % 2), row))
    stiff_other = send(stiff[0], to_core)
    aux_other = send(after(aux, stiff_other), to_core)
    mass_part, masked, spots = call(
        mass_kernel,
        [shape(128, 256), shape(2048, 128, dtype=BF16), shape(8, 128, dtype=jnp.int32)],
        [both, aux, aux_other],
        [],
        [pltpu.VMEM((2048, 128), F32)],
    )
    left2, right2 = send(left1, ring(True)), send(right1, ring(False))
    go, keep = call(
        early_kernel,
        [shape(192, 256)] * 2,
        [both, partner, mass_part, masked, spots],
        [],
        [pltpu.VMEM((2048, 256), BF16), pltpu.SMEM((8, 128), jnp.int32), pltpu.SemaphoreType.DMA],
        flops=2**30,
        vmem=16,
    )
    left3, right3 = send(left2, ring(True)), send(after(right2, go), ring(False))
    left4 = send(left3, ring(True))
    came = send(go, to_side)
    go, keep = call(turn_kernel, [shape(64, 256), shape(128, 256)], [keep, came], flops=0 * 10**9)
    came = send(go, to_core)
    go, early_keep = call(split_kernel, [shape(96, 256)] * 2, [keep, came], flops=4 * 10**9)
    early_came = send(go, to_group(1))

    table, matrix, start, spots = call(
        stage_kernel,
        [shape(16384, 128, dtype=BF16), shape(2048, 1664, dtype=BF16), shape(2048, 128), shape(32, 128, dtype=jnp.int32)],
        [both, aux, aux_other],
        [kcols, stiff, stiff_other, half, left1, right1, left2, right2, left3, right3],
        [pltpu.VMEM((1, 16, 26), jnp.int32), pltpu.SemaphoreType.DMA((10,))],
    )
    go, keep, _ = call(
        own_kernel,
        [shape(64, 256), shape(64, 256), shape(16384, 128, dtype=BF16)],
        [table, matrix, start, spots, both],
        [left4],
        [pltpu.VMEM((2048, 128), BF16), pltpu.SMEM((32, 128), jnp.int32), pltpu.SemaphoreType.DMA((2,))],
        flops=2**30,
        aliases={0: 2},
    )
    came = send(go, to_side)
    total, pay, base, mass_base = call(
        gather_kernel,
        [shape(64, 256), shape(80, 256), shape(64, 256), shape(16, 256)],
        [keep, came, early_keep, early_came],
    )
    one = send(total, to_own_group(1))
    three = send(total, to_own_group(3))
    two = send(pay, to_group(2))
    kred, mred = call(last_kernel, [shape(64, 256), shape(16, 256)], [base, mass_base, one, two, three])
    return (kred.T[None], mred.T[None])


def solution(mesh):
    in_specs = (
        P("leaf", "rows", None),
        P("leaf", "rows", None),
        P("leaf", "rows", None),
        P("leaf", "rows", None),
        P("leaf", "rows", None),
        P("leaf", "rows"),
        P("leaf", "rows"),
    )
    out_specs = (P("leaf", None, "rows"), P("leaf", None, "rows"))
    return jax.shard_map(shards, mesh=mesh, in_specs=in_specs, out_specs=out_specs, check_vma=False)
```

```python
import functools

import jax
import jax.numpy as jnp
from jax import lax
from jax.experimental import pallas as pl
from jax.experimental.pallas import tpu as pltpu
from jax.sharding import PartitionSpec as P

F32, BF16 = jnp.float32, jnp.bfloat16
BLK = 64
MIB = 2**20
COUPLE, SHIFT, MASS, KCOLS, LINKS, AUX = 0, 1024, 1032, 1040, 1056, 1072
VMEM = pl.BlockSpec(memory_space=pltpu.VMEM)
SMEM = pl.BlockSpec(memory_space=pltpu.SMEM)
ANY = pl.BlockSpec(memory_space=pl.ANY)
HBM = pl.BlockSpec(memory_space=pltpu.HBM)


def place():
    row = lax.axis_index("rows")
    return row // 4, (row // 2) % 2, row % 2


def send(value, to):
    leaves, rows = lax.axis_size("leaf"), lax.axis_size("rows")
    pairs = []
    for leaf in range(leaves):
        for row in range(rows):
            target = to(leaf, row)
            if target is not None:
                pairs.append((leaf * rows + row, target[0] * rows + target[1]))
    return lax.ppermute(value, ("leaf", "rows"), pairs)


def to_core(leaf, row):
    return leaf, row ^ 1


def to_side(leaf, row):
    return leaf, row ^ 2


def ring(forward):
    def to(leaf, row):
        step = 2 if (row % 2 == 0) == forward else -2
        return leaf, (row + step) % 16

    return to


def to_group(mask):
    return lambda leaf, row: (leaf, row ^ (4 * mask))


def to_own_group(mask):
    def to(leaf, row):
        return (leaf, 4 * (leaf % 4) + row % 4) if row // 4 == (leaf % 4) ^ mask else None

    return to


def call(body, outs, arrays, far=(), scratch=(), flops=0, vmem=8, aliases=None):
    moved = sum(x.size * x.dtype.itemsize for x in [*arrays, *far, *outs])
    return pl.pallas_call(
        body,
        out_shape=outs,
        in_specs=[VMEM] * len(arrays) + [HBM] * len(far),
        out_specs=[VMEM] * len(outs),
        scratch_shapes=list(scratch),
        input_output_aliases=aliases or {},
        compiler_params=pltpu.CompilerParams(vmem_limit_bytes=vmem * MIB),
        cost_estimate=pl.CostEstimate(flops=flops, bytes_accessed=moved, transcendentals=0),
    )(*arrays, *far)


def fetch(pairs, sems):
    copies = [pltpu.make_async_copy(src, dst, sems.at[n]) for n, (src, dst) in enumerate(pairs)]
    for copy in copies:
        copy.start()
    return copies


def shape(*dims, dtype=F32):
    return jax.ShapeDtypeStruct(dims, dtype)


def mine_of(width, column):
    here = lax.broadcasted_iota(jnp.int32, (width, 128), 0)
    want = column(lax.broadcasted_iota(jnp.int32, (width, 128), 1))
    return (here == want).astype(F32).astype(BF16)


def dot(a, b):
    return jnp.dot(a, b, preferred_element_type=F32)


def dot_t(a, b):
    return lax.dot_general(a, b, (((0,), (0,)), ((), ())), preferred_element_type=F32)


def after(value, *others):
    return lax.optimization_barrier((value, *others))[0]


def aux_kernel(couple_at, kcols_at, links_at, shift_at, mass_at, out, couple, kcols, links, shift, mass, sems):
    held = (couple, kcols, links, shift, mass)
    for copy in fetch(zip((couple_at, kcols_at, links_at, shift_at, mass_at), held), sems):
        copy.wait()
    out[COUPLE : COUPLE + 1024, :] = couple[0].astype(F32)
    for k in range(8):
        out[SHIFT + k : SHIFT + k + 1, :] = shift[:, k * 128 : (k + 1) * 128]
        out[MASS + k : MASS + k + 1, :] = mass[:, k * 128 : (k + 1) * 128]
    out[KCOLS:AUX, :] = jnp.zeros((AUX - KCOLS, 128), F32)
    out[KCOLS : KCOLS + 16, 0:26] = kcols[0].astype(F32)
    out[LINKS : LINKS + 2, 0:16] = links[0].astype(F32)


def mine(core):
    return mine_of(256, lambda n: 64 * core + n + jnp.where(n >= 64, 64, 0))


def first_kernel(own, held, half):
    _, _, core = place()
    held[...] = own[...]
    half[...] = dot(own[...], mine(core)).astype(BF16)


def half_kernel(own, own_half, other, out, both):
    _, _, core = place()
    out[pl.ds(pl.multiple_of(core * 1024, 1024), 1024), :] = own_half[...]
    out[pl.ds(pl.multiple_of((1 - core) * 1024, 1024), 1024), :] = dot(other[...], mine(core)).astype(BF16)
    both[0:1024, :] = own[...]
    both[1024:2048, :] = other[...]


def spread(dst, rows_own, rows_other):
    for part, rows in enumerate((rows_own, rows_other)):
        turned = jnp.transpose(jnp.concatenate([rows, jnp.zeros((120, 128), F32)], axis=0))
        for k in range(8):
            dst[part * 1024 + k * 128 : part * 1024 + (k + 1) * 128, :] = jnp.broadcast_to(
                turned[:, k : k + 1], (128, 128)
            )


def mass_kernel(both, aux, aux_other, mred, masked, spots, weights):
    _, _, core = place()
    spread(weights, aux[MASS : MASS + 8, :], aux_other[MASS : MASS + 8, :])
    pick = mine_of(256, lambda n: 64 * ((n % 64) // 16) + 32 * (n // 64) + 16 * core + n % 16)
    weighted = (weights[...] * dot(both[...], pick)).astype(BF16)
    mred[...] = dot_t(weighted, both[...])
    spots[...] = jnp.zeros((8, 128), jnp.int32)
    here = lax.broadcasted_iota(jnp.int32, (1024, 128), 1) // BLK == core
    for part, rows in enumerate((aux, aux_other)):
        links = rows[LINKS : LINKS + 2, 0:16].astype(jnp.int32)
        spots[part : part + 1, 0:16] = part * 1024 + jnp.where(core == 0, links[0:1, :], links[1:2, :]) * BLK
        couple = rows[COUPLE : COUPLE + 1024, :]
        masked[part * 1024 : (part + 1) * 1024, :] = jnp.where(here, couple, 0.0).astype(BF16)


def early_kernel(both, partner, mred, masked, spots, to_send, to_keep, coupled, at, sem):
    _, side, _ = place()
    copy = pltpu.make_async_copy(spots, at, sem)
    copy.start()
    copy.wait()

    def one(b, carry):
        rows = pl.ds(pl.multiple_of(b * BLK, BLK), BLK)
        block = partner[pl.ds(pl.multiple_of(at[b // 16, b % 16], BLK), BLK), :]
        coupled[rows, :] = dot(masked[rows, :], jnp.concatenate([block, block], axis=0)).astype(BF16)
        return carry

    lax.fori_loop(0, 32, one, 0, unroll=16)
    term = dot_t(coupled[...], both[...])
    for low, high, rows in (
        (term[0:128, :], term[128:256, :], slice(0, 128)),
        (mred[0:64, :], mred[64:128, :], slice(128, 192)),
    ):
        to_send[rows, :] = jnp.where(side == 0, high, low)
        to_keep[rows, :] = jnp.where(side == 0, low, high)


def turn_kernel(kept, came, to_send, to_keep):
    _, _, core = place()
    total = kept[...] + came[...]
    to_send[...] = jnp.where(core == 0, total[64:128, :], total[0:64, :])
    to_keep[0:64, :] = jnp.where(core == 0, total[0:64, :], total[64:128, :])
    to_keep[64:128, :] = total[128:192, :]


def split_kernel(kept, came, to_send, to_keep):
    group, _, core = place()
    odd = (group ^ (lax.axis_index("leaf") % 4)) % 2 == 1
    sib = jnp.where(core == 0, kept[0:64, :], came[...])
    cous = jnp.where(core == 0, came[...], kept[0:64, :])
    mass = kept[64:128, :]
    to_keep[0:64, :] = jnp.where(odd, sib, cous)
    to_send[0:64, :] = jnp.where(odd, cous, sib)
    low = group % 2 == 0
    for k in range(2):
        even, uneven = mass[k * 32 : k * 32 + 16, :], mass[k * 32 + 16 : k * 32 + 32, :]
        to_keep[64 + k * 16 : 80 + k * 16, :] = jnp.where(low, even, uneven)
        to_send[64 + k * 16 : 80 + k * 16, :] = jnp.where(low, uneven, even)


def stage_kernel(both, aux, aux_other, *refs):
    kcols_at, stiff, stiff_other = refs[:3]
    pieces = refs[3:10]
    table, matrix, start, spots, kcols, sems = refs[10:]
    _, _, core = place()
    chip = lax.axis_index("rows") // 2
    places = [2048 * d for d in (0, 7, 1, 6, 2, 5, 3)]
    pairs = [(kcols_at, kcols), (pieces[0], table.at[0:2048, :])]
    pairs += [(piece, table.at[lo : lo + 2048, :]) for piece, lo in list(zip(pieces, places))[1:]]
    pairs += [(stiff.at[0], matrix.at[0:1024, :]), (stiff_other, matrix.at[1024:2048, :])]
    copies = fetch(pairs, sems)
    spread(start, aux[SHIFT : SHIFT + 8, :], aux_other[SHIFT : SHIFT + 8, :])
    copies[0].wait()
    copies[1].wait()
    spots[...] = jnp.zeros((32, 128), jnp.int32)
    for part in range(2):
        column = kcols[0] if part == 0 else aux_other[KCOLS : KCOLS + 16, 0:26].astype(jnp.int32)
        ahead = column // 32 - chip
        ahead = jnp.where(core == 0, ahead, -ahead) & 7
        spots[part * 16 : (part + 1) * 16, 0:26] = ahead * 2048 + (column % 32) * BLK
    for part in range(2):
        rows = slice(part * 1024, (part + 1) * 1024)
        mine = pl.ds(pl.multiple_of((part * 1024 + core * 1024) % 2048, 1024), 1024)
        start[rows, :] = start[rows, :] * table[mine, :].astype(F32)
    for copy in copies[2:]:
        copy.wait()


def own_kernel(table, matrix, start, spots, both, last_at, to_send, to_keep, full, image, at, sems):
    _, side, _ = place()
    copies = fetch([(spots, at), (last_at, full.at[4 * 2048 : 5 * 2048, :])], sems)
    for copy in copies:
        copy.wait()

    def one(b, carry):
        rows = pl.ds(pl.multiple_of(b * BLK, BLK), BLK)
        total = start[rows, :]
        blocks = [full[pl.ds(pl.multiple_of(at[b, k], BLK), BLK), :] for k in range(26)]
        for g in range(0, 26, 4):
            picked = jnp.concatenate(blocks[g : g + 4], axis=0)
            width = picked.shape[0]
            total += dot(matrix[rows, g * BLK : g * BLK + width], picked)
        image[rows, :] = total.astype(BF16)
        return carry

    lax.fori_loop(0, 32, one, 0, unroll=16)
    result = dot_t(image[...], both[...])
    low, high = result[0:64, :], result[64:128, :]
    to_send[...] = jnp.where(side == 0, high, low)
    to_keep[...] = jnp.where(side == 0, low, high)


def gather_kernel(kept, came, early_kept, early_came, total, pay, base, mass_base):
    group, _, _ = place()
    term = group ^ (lax.axis_index("leaf") % 4)
    own = kept[...] + came[...]
    early = early_kept[0:64, :] + early_came[0:64, :]
    total[0:64, :] = own
    total[64:88, :] = own[0:24, :]
    zero = jnp.zeros_like(own)
    pay[0:64, :] = jnp.where(term == 2, own, jnp.where(term == 1, zero, early))
    base[...] = jnp.where(term == 0, own, jnp.where(term == 3, zero, early))
    first = early_kept[64:80, :] + early_came[64:80, :]
    second = early_kept[80:96, :] + early_came[80:96, :]
    low = group < 2
    pay[64:80, :] = jnp.where(low, second, first)
    mass_base[...] = jnp.where(low, first, second)


def last_kernel(base, mass_base, one, two, three, kred, mred):
    kred[...] = base[...] + one[0:64, :] + two[0:64, :] + three[0:64, :]
    mred[...] = mass_base[...] + two[64:80, :]


def shards(basis, stiff, kcols, couple, links, shift, mass):
    own = basis[0]
    links = links.transpose(0, 2, 1)
    other = send(own, to_core)
    own_held, own_half = call(first_kernel, [shape(1024, 256, dtype=BF16), shape(1024, 128, dtype=BF16)], [own])
    half, both = call(
        half_kernel,
        [shape(2048, 128, dtype=BF16), shape(2048, 256, dtype=BF16)],
        [own_held, own_half, other],
        flops=4 * 10**10,
    )
    left1 = send(half, ring(True))
    (aux,) = call(
        aux_kernel,
        [shape(AUX, 128)],
        [],
        [couple, after(kcols, own_held), links, shift, mass],
        [
            pltpu.VMEM((1, 1024, 128), BF16),
            pltpu.VMEM((1, 16, 26), jnp.int32),
            pltpu.VMEM((1, 2, 16), jnp.int32),
            pltpu.VMEM((1, 1024), F32),
            pltpu.VMEM((1, 1024), F32),
            pltpu.SemaphoreType.DMA((5,)),
        ],
        vmem=56,
    )
    right1 = send(half, ring(False))
    partner = send(both, lambda leaf, row: (leaf ^ (1 + row % 2), row))
    stiff_other = send(stiff[0], to_core)
    aux_other = send(after(aux, stiff_other), to_core)
    mass_part, masked, spots = call(
        mass_kernel,
        [shape(128, 256), shape(2048, 128, dtype=BF16), shape(8, 128, dtype=jnp.int32)],
        [both, aux, aux_other],
        [],
        [pltpu.VMEM((2048, 128), F32)],
    )
    left2, right2 = send(left1, ring(True)), send(right1, ring(False))
    go, keep = call(
        early_kernel,
        [shape(192, 256)] * 2,
        [both, partner, mass_part, masked, spots],
        [],
        [pltpu.VMEM((2048, 256), BF16), pltpu.SMEM((8, 128), jnp.int32), pltpu.SemaphoreType.DMA],
        flops=2**30,
        vmem=16,
    )
    left3, right3 = send(left2, ring(True)), send(after(right2, go), ring(False))
    left4 = send(left3, ring(True))
    came = send(go, to_side)
    go, keep = call(turn_kernel, [shape(64, 256), shape(128, 256)], [keep, came], flops=0 * 10**9)
    came = send(go, to_core)
    go, early_keep = call(split_kernel, [shape(96, 256)] * 2, [keep, came], flops=4 * 10**9)
    early_came = send(go, to_group(1))

    table, matrix, start, spots = call(
        stage_kernel,
        [shape(16384, 128, dtype=BF16), shape(2048, 1664, dtype=BF16), shape(2048, 128), shape(32, 128, dtype=jnp.int32)],
        [both, aux, aux_other],
        [kcols, stiff, stiff_other, half, left1, right1, left2, right2, left3, right3],
        [pltpu.VMEM((1, 16, 26), jnp.int32), pltpu.SemaphoreType.DMA((10,))],
    )
    go, keep, _ = call(
        own_kernel,
        [shape(64, 256), shape(64, 256), shape(16384, 128, dtype=BF16)],
        [table, matrix, start, spots, both],
        [left4],
        [pltpu.VMEM((2048, 128), BF16), pltpu.SMEM((32, 128), jnp.int32), pltpu.SemaphoreType.DMA((2,))],
        flops=2**30,
        aliases={0: 2},
    )
    came = send(go, to_side)
    total, pay, base, mass_base = call(
        gather_kernel,
        [shape(88, 256), shape(80, 256), shape(64, 256), shape(16, 256)],
        [keep, came, early_keep, early_came],
    )
    one = send(total, to_own_group(1))
    three = send(total, to_own_group(3))
    two = send(pay, to_group(2))
    kred, mred = call(last_kernel, [shape(64, 256), shape(16, 256)], [base, mass_base, one, two, three])
    return (kred.T[None], mred.T[None])


def solution(mesh):
    in_specs = (
        P("leaf", "rows", None),
        P("leaf", "rows", None),
        P("leaf", "rows", None),
        P("leaf", "rows", None),
        P("leaf", "rows", None),
        P("leaf", "rows"),
        P("leaf", "rows"),
    )
    out_specs = (P("leaf", None, "rows"), P("leaf", None, "rows"))
    return jax.shard_map(shards, mesh=mesh, in_specs=in_specs, out_specs=out_specs, check_vma=False)
```
